128 devices in a mesh: atm: 8 (over y, core), ocn: 16 (over x, z).
Axes of the slice: x: 4, y: 4, z: 4, core: 2. Of those that a mesh axis runs over, the one named last changes fastest.
Arguments:
- atm_fields: bfloat16 [65536, 4, 8, 64], P(('atm', 'ocn')), may hold values from -6 to 6
- requests: int32 [128, 128, 6], P(('atm', 'ocn')), may hold values from 0 to 65535, as said below
- ocean_block: int32 [128, 128, 6], P(('atm', 'ocn')), may hold values from 0 to 511
- live_counts: int32 [128, 128], P(('atm', 'ocn')), may hold values from 0 to 6, as said below
- weights: bfloat16 [128, 128, 6, 64, 64], P(('atm', 'ocn')), may hold values from -0.75 to 0.75
Outputs:
- remapped: float32 [65536, 4, 8, 64], P(('atm', 'ocn'))
The draws below stay inside these ranges and needn't reach their ends.
Inputs may be any that keep to these rules, and one draw needn't show every extreme that they name: requests[d,s,k] names a block of owner s: s*512 <= requests[d,s,k] < (s+1)*512. `live_counts`: every ocean owner has exactly 6 live slots from some source owner.
All inputs are finite; a program needn't handle non-finite values.
Results may differ from the reference program's by a relative error of at most 0.0003.
Values may be sent and summed in bfloat16 or wider, within the bound.
A program may use at most 128 MiB of HBM per device.

```python
import jax
import jax.numpy as jnp
from jax import lax

F = 8
BLK = 64
NT = 4
AB_DEV = 512
OB_DEV = 512
OWNERS = 128
CAP = 6
ABLK = 65536
OBLK = 65536


def draw_requests(key, part):
    key = jax.random.fold_in(key, 11)
    local = jax.random.randint(key, (OWNERS, OWNERS, CAP), 0, AB_DEV)
    source = lax.broadcasted_iota(jnp.int32, (OWNERS, OWNERS, CAP), 1)
    return (source * AB_DEV + local).astype(jnp.int32)


def draw_live_counts(key, part):
    key = jax.random.fold_in(key, 23)
    first, second, third = jax.random.split(key, 3)
    counts = jax.random.randint(first, (OWNERS, OWNERS), 0, CAP + 1)
    full = jax.random.randint(second, (OWNERS, OWNERS), 0, 2)
    counts = jnp.where(full == 1, CAP, counts)
    chosen = jax.random.randint(third, (OWNERS, 1), 0, OWNERS)
    column = lax.broadcasted_iota(jnp.int32, (OWNERS, OWNERS), 1)
    return jnp.where(column == chosen, CAP, counts).astype(jnp.int32)


def touch_ends(array, stream_key, least, top_value):
    longest = array.shape.index(max(array.shape))
    spots = []
    for shift in (0, 1):
        where = [jax.random.randint(jax.random.fold_in(stream_key, axis), (), 0, length) for axis, length in enumerate(array.shape)]
        where[longest] = (where[longest] + shift) % array.shape[longest]
        spots.append(tuple(where))
    return array.at[spots[0]].set(least).at[spots[1]].set(top_value)


def steps_of(rng, extent, pieces, low, high):
    def one(axis_at, shards_of):
        heights = jax.random.uniform(jax.random.fold_in(jax.random.fold_in(rng, 6), axis_at), (shards_of,), jnp.float32, low / len(pieces), high / len(pieces))
        return jnp.repeat(jnp.exp(heights), extent[axis_at] // shards_of).reshape((-1,) + (1,) * (len(extent) - axis_at - 1))

    gain = one(*pieces[0])
    for cut in pieces[1:]:
        gain = gain * one(*cut)
    return gain


def normal_values(stream_key, extent, deviation, most, cuts=(), dtype=jnp.bfloat16):
    values = deviation * jax.random.normal(stream_key, extent, jnp.float32)
    if cuts:
        values = values * steps_of(stream_key, extent, cuts, -0.22, 0.18)
    return jnp.clip(values, -most, most).astype(dtype)


def setup_inputs(seed: int = 0) -> dict:
    seeds = jax.random.split(jax.random.key(seed), 6)
    return {
        "atm_fields": normal_values(seeds[0], (ABLK, NT, F, BLK), 1.0, 6.0, ((0, 128),)),
        "requests": draw_requests(jax.random.fold_in(seeds[5], 71), 0),
        "ocean_block": touch_ends(jax.random.randint(seeds[2], (OWNERS, OWNERS, CAP), 0, OB_DEV), jax.random.fold_in(seeds[2], 1), 0, OB_DEV - 1).astype(jnp.int32),
        "live_counts": draw_live_counts(jax.random.fold_in(seeds[5], 71), 0),
        "weights": normal_values(seeds[4], (OWNERS, OWNERS, CAP, BLK, BLK), BLK ** -0.5, 0.75, ((0, 128),)),
    }


def reference(atm_fields, requests, ocean_block, live_counts, weights):
    slot = lax.broadcasted_iota(jnp.int32, (OWNERS, CAP), 1)
    flat_fields = atm_fields.reshape(ABLK, NT * F, BLK)

    def one_owner(args):
        wanted, targets, counts, mats = args
        data = flat_fields[wanted.reshape(-1)].astype(jnp.float32)
        square = mats.reshape(OWNERS * CAP, BLK, BLK).astype(jnp.float32)
        part = jnp.einsum("sra,sao->sro", data, square)
        alive = (slot < counts[:, None]).reshape(-1)
        part = jnp.where(alive[:, None, None], part, jnp.float32(0.0))
        return jax.ops.segment_sum(part, targets.reshape(-1).astype(jnp.int32), num_segments=OB_DEV)

    result = lax.map(one_owner, (requests, ocean_block, live_counts, weights))
    return result.reshape(OBLK, NT, F, BLK)
```

```python
import jax
import jax.numpy as jnp
from jax import lax
from jax.experimental import pallas as pl
from jax.experimental.pallas import tpu as pltpu
from jax.sharding import PartitionSpec as P

MESH = pl.DeviceIdType.MESH
OWNERS = 128
NATM = 8
NOCN = 16
CAP = 6
PAIRS = 3
CELLS = 64
TF = 32
HALF = 16
NBLK = 512
GROUPS = 8
PER = OWNERS // GROUPS
ROWS = PAIRS * TF
WPITCH = CELLS


def shift_of(i):
    j = (i * 37) % OWNERS
    return j // 32, (j // 16) % 2, (j // 4) % 4, j % 4


def moved(i, sign):
    atm = lax.axis_index("atm")
    ocn = lax.axis_index("ocn")
    dy, dc, dx, dz = shift_of(i)
    y = (atm // 2 + 4 + sign * dy) % 4
    c = (atm % 2 + 2 + sign * dc) % 2
    x = (ocn // 4 + 4 + sign * dx) % 4
    z = (ocn % 4 + 4 + sign * dz) % 4
    return y * 2 + c, x * 4 + z


def exchange_kernel(
    x_hbm, req_ref, w_hbm, out_ref,
    xin, win, xt, wt, reqrow, r1, r2, idx, send, recv,
    xsem, wsem, lsem, s1, v1, s2, v2, dsend, drecv,
):
    atm = lax.axis_index("atm")
    ocn = lax.axis_index("ocn")
    xcopy = pltpu.make_async_copy(x_hbm, xin, xsem)
    xcopy.start()
    wcopy = pltpu.make_async_copy(w_hbm, win, wsem)
    wcopy.start()

    barrier = pltpu.get_barrier_semaphore()

    def greet_atm(i, carry):
        pl.semaphore_signal(barrier, inc=1, device_id=((atm + i) % NATM, ocn), device_id_type=MESH)
        return carry

    def greet_ocn(i, carry):
        pl.semaphore_signal(barrier, inc=1, device_id=(atm, (ocn + i) % NOCN), device_id_type=MESH)
        return carry

    lax.fori_loop(1, NATM, greet_atm, 0)
    lax.fori_loop(1, NOCN, greet_ocn, 0)

    padded = jnp.concatenate([req_ref[...] & (NBLK - 1), jnp.zeros((OWNERS - CAP, OWNERS), jnp.int32)], axis=0)
    turned = jnp.transpose(padded)
    for s in range(OWNERS):
        reqrow[s // NOCN, s % NOCN] = turned[s : s + 1, :]

    pl.semaphore_wait(barrier, NATM + NOCN - 2)

    def first_hop(i, carry):
        to = (atm + i) % NATM
        pltpu.make_async_remote_copy(
            reqrow.at[to], r1.at[atm], s1, v1, device_id=(to, ocn), device_id_type=MESH
        ).start()
        return carry

    lax.fori_loop(1, NATM, first_hop, 0)
    own = pltpu.make_async_copy(reqrow.at[atm], r1.at[atm], lsem)
    own.start()

    xcopy.wait()
    xflat = xt.reshape(NBLK * HALF, 2 * CELLS)

    def turn_fields(tp, carry):
        both = jnp.concatenate([xin[tp], xin[tp + HALF]], axis=0).astype(jnp.float32)
        for b in range(0, NBLK, 128):
            xflat[pl.ds(b * HALF + tp, 128, stride=HALF), :] = jnp.transpose(both[:, b : b + 128])
        return carry

    lax.fori_loop(0, HALF // 2, turn_fields, 0)

    own.wait()
    hop1 = pltpu.make_async_remote_copy(
        reqrow.at[pl.ds(0, NATM - 1)], r1.at[pl.ds(0, NATM - 1)], s1, v1,
        device_id=(atm, ocn), device_id_type=MESH,
    )
    hop1.wait_recv()

    def second_hop(i, carry):
        to = (ocn + i) % NOCN
        pltpu.make_async_remote_copy(
            r1.at[:, to], r2.at[ocn], s2, v2, device_id=(atm, to), device_id_type=MESH
        ).start()
        return carry

    lax.fori_loop(1, NOCN, second_hop, 0)
    own2 = pltpu.make_async_copy(r1.at[:, ocn], r2.at[ocn], lsem)
    own2.start()

    lax.fori_loop(HALF // 2, HALF, turn_fields, 0)

    own2.wait()
    hop1.wait_send()
    hop2 = pltpu.make_async_remote_copy(
        r2.at[pl.ds(0, NOCN - 1)], r2.at[pl.ds(0, NOCN - 1)], s2, v2,
        device_id=(atm, ocn), device_id_type=MESH,
    )
    hop2.wait_recv()
    hop2.wait_send()
    tosmem = pltpu.make_async_copy(r2, idx, lsem)
    tosmem.start()
    tosmem.wait()

    left = lax.broadcasted_iota(jnp.int32, (HALF, 2 * CELLS), 1) < CELLS

    def fill(i, box, at):
        ta, to = moved(i, 1)
        for p in range(PAIRS):
            ia = idx[to, ta, 0, 2 * p]
            ib = idx[to, ta, 0, 2 * p + 1]
            a = xt[ia]
            b = xt[ib]
            low = jnp.where(left, a, pltpu.roll(b, CELLS, 1))
            high = jnp.where(left, pltpu.roll(a, CELLS, 1), b)
            box[at, p * TF : p * TF + HALF, :] = low.astype(jnp.bfloat16)
            box[at, p * TF + HALF : (p + 1) * TF, :] = high.astype(jnp.bfloat16)
        return ta, to

    fill(0, recv, 0)

    def ship(i, carry):
        ta, to = fill(i, send, i)
        pltpu.make_async_remote_copy(
            send.at[i], recv.at[i], dsend, drecv.at[i // PER],
            device_id=(ta, to), device_id_type=MESH,
        ).start()
        return carry

    lax.fori_loop(1, OWNERS, ship, 0)

    wcopy.wait()
    for p in range(PAIRS):
        def turn_weights(a, carry):
            both = jnp.concatenate([win[2 * p, a], win[2 * p + 1, a]], axis=0).astype(jnp.float32)
            wt[p, pl.ds(a, OWNERS, stride=WPITCH), :] = jnp.transpose(both)
            return carry

        lax.fori_loop(0, CELLS, turn_weights, 0)

    lane = lax.broadcasted_iota(jnp.int32, (CELLS, 2 * CELLS), 1) < CELLS

    def apply(i, carry):
        fa, fo = moved(i, -1)
        s = fa * NOCN + fo
        for p in range(PAIRS):
            w = wt[p, pl.ds(pl.multiple_of(s * WPITCH, 8), CELLS), :]
            zero = jnp.zeros_like(w)
            square = jnp.concatenate([jnp.where(lane, w, zero), jnp.where(lane, zero, w)], axis=0).astype(jnp.bfloat16)
            part = jnp.dot(recv[i, p * TF : (p + 1) * TF, :], square, preferred_element_type=jnp.float32)
            out_ref[pl.ds(p * OWNERS + s, TF, stride=PAIRS * OWNERS), :] = part
        return carry

    for g in range(GROUPS):
        n = PER - 1 if g == 0 else PER
        pltpu.make_async_remote_copy(
            send.at[pl.ds(0, n)], recv.at[pl.ds(0, n)], dsend, drecv.at[g],
            device_id=(atm, ocn), device_id_type=MESH,
        ).wait_recv()
        lax.fori_loop(g * PER, (g + 1) * PER, apply, 0)

    pltpu.make_async_remote_copy(
        send.at[pl.ds(1, OWNERS - 1)], recv.at[pl.ds(1, OWNERS - 1)], dsend, drecv.at[0],
        device_id=(atm, ocn), device_id_type=MESH,
    ).wait_send()


def exchange(fields, req, mats):
    big = pl.BlockSpec(memory_space=pl.ANY)
    vmem = pl.BlockSpec(memory_space=pltpu.VMEM)
    return pl.pallas_call(
        exchange_kernel,
        out_shape=jax.ShapeDtypeStruct((TF * PAIRS * OWNERS, 2 * CELLS), jnp.float32),
        in_specs=[big, vmem, big],
        out_specs=vmem,
        scratch_shapes=[
            pltpu.VMEM((TF, CELLS, NBLK), jnp.bfloat16),
            pltpu.VMEM((CAP, CELLS, CELLS, OWNERS), jnp.bfloat16),
            pltpu.VMEM((NBLK, HALF, 2 * CELLS), jnp.float32),
            pltpu.VMEM((PAIRS, OWNERS * WPITCH, 2 * CELLS), jnp.float32),
            pltpu.VMEM((NATM, NOCN, 1, 128), jnp.int32),
            pltpu.VMEM((NATM, NOCN, 1, 128), jnp.int32),
            pltpu.VMEM((NOCN, NATM, 1, 128), jnp.int32),
            pltpu.SMEM((NOCN, NATM, 1, 128), jnp.int32),
            pltpu.VMEM((OWNERS, ROWS, 2 * CELLS), jnp.bfloat16),
            pltpu.VMEM((OWNERS, ROWS, 2 * CELLS), jnp.bfloat16),
            pltpu.SemaphoreType.DMA,
            pltpu.SemaphoreType.DMA,
            pltpu.SemaphoreType.DMA,
            pltpu.SemaphoreType.DMA,
            pltpu.SemaphoreType.DMA,
            pltpu.SemaphoreType.DMA,
            pltpu.SemaphoreType.DMA,
            pltpu.SemaphoreType.DMA,
            pltpu.SemaphoreType.DMA((GROUPS,)),
        ],
        compiler_params=pltpu.CompilerParams(
            collective_id=0, has_side_effects=True, vmem_limit_bytes=56 << 20
        ),
        name="exchange",
    )(fields, req, mats)


def place_kernel(p_ref, tgt_ref, cnt_ref, o_ref, hot, lhs):
    @pl.when(pl.program_id(0) == 0)
    def _():
        block = lax.broadcasted_iota(jnp.int32, (NBLK, OWNERS), 0)
        for par in range(2):
            for p in range(PAIRS):
                k = 2 * p + par
                live = jnp.where(cnt_ref[...] > k, tgt_ref[k : k + 1, :], -1)
                at = (par * PAIRS + p) * OWNERS
                hot[:, at : at + OWNERS] = jnp.where(block == live, 1.0, 0.0).astype(jnp.bfloat16)

    nf = p_ref.shape[0]
    for f in range(nf):
        turned = jnp.transpose(p_ref[f])
        rows = jnp.concatenate([turned[:CELLS], turned[CELLS:]], axis=1)
        high = rows.astype(jnp.bfloat16)
        low = (rows - high.astype(jnp.float32)).astype(jnp.bfloat16)
        lhs[f * CELLS : (f + 1) * CELLS, :] = high
        lhs[(nf + f) * CELLS : (nf + f + 1) * CELLS, :] = low
    both = lax.dot_general(
        lhs[...], hot[...], (((1,), (1,)), ((), ())), preferred_element_type=jnp.float32
    )
    total = both[: nf * CELLS] + both[nf * CELLS :]
    o_ref[...] = total.reshape(nf, CELLS, NBLK)


def place(parts, targets, counts):
    nf = 8
    return pl.pallas_call(
        place_kernel,
        grid=(TF // nf,),
        out_shape=jax.ShapeDtypeStruct((TF, CELLS, NBLK), jnp.float32),
        in_specs=[
            pl.BlockSpec((nf, PAIRS * OWNERS, 2 * CELLS), lambda t: (t, 0, 0)),
            pl.BlockSpec((CAP, OWNERS), lambda t: (0, 0)),
            pl.BlockSpec((1, OWNERS), lambda t: (0, 0)),
        ],
        out_specs=pl.BlockSpec((nf, CELLS, NBLK), lambda t: (t, 0, 0)),
        scratch_shapes=[
            pltpu.VMEM((NBLK, 2 * PAIRS * OWNERS), jnp.bfloat16),
            pltpu.VMEM((2 * nf * CELLS, 2 * PAIRS * OWNERS), jnp.bfloat16),
        ],
        compiler_params=pltpu.CompilerParams(vmem_limit_bytes=48 << 20),
        name="place",
    )(parts, targets, counts)


def on_device(atm_fields, requests, ocean_block, live_counts, weights):
    fields = jnp.transpose(atm_fields, (1, 2, 3, 0)).reshape(TF, CELLS, NBLK)
    req = jnp.transpose(requests[0])
    targets = jnp.transpose(ocean_block[0])
    mats = jnp.transpose(weights[0], (1, 2, 3, 0))
    parts = exchange(fields, req, mats)
    out = place(parts.reshape(TF, PAIRS * OWNERS, 2 * CELLS), targets, live_counts)
    return jnp.transpose(out.reshape(4, 8, CELLS, NBLK), (3, 0, 1, 2))


def solution(mesh):
    in_specs = (
        P(("atm", "ocn"), None, None, None),
        P(("atm", "ocn"), None, None),
        P(("atm", "ocn"), None, None),
        P(("atm", "ocn"), None),
        P(("atm", "ocn"), None, None, None, None),
    )
    out_specs = P(("atm", "ocn"), None, None, None)
    return jax.shard_map(
        on_device, mesh=mesh, in_specs=in_specs, out_specs=out_specs, check_vma=False
    )
```

```python
import jax
import jax.numpy as jnp
from jax import lax
from jax.experimental import pallas as pl
from jax.experimental.pallas import tpu as pltpu
from jax.sharding import PartitionSpec as P

MESH = pl.DeviceIdType.MESH
OWNERS = 128
NATM = 8
NOCN = 16
CAP = 6
KROWS = 8
PAIRS = 3
CELLS = 64
TF = 32
HALF = 16
NBLK = 512
GROUPS = 16
PER = OWNERS // GROUPS
ROWS = PAIRS * TF
WPITCH = CELLS


def shift_of(i):
    j = (i * 37) % OWNERS
    return j // 32, (j // 16) % 2, (j // 4) % 4, j % 4


def moved(i, sign):
    atm = lax.axis_index("atm")
    ocn = lax.axis_index("ocn")
    dy, dc, dx, dz = shift_of(i)
    y = (atm // 2 + 4 + sign * dy) % 4
    c = (atm % 2 + 2 + sign * dc) % 2
    x = (ocn // 4 + 4 + sign * dx) % 4
    z = (ocn % 4 + 4 + sign * dz) % 4
    return y * 2 + c, x * 4 + z


def exchange_kernel(
    x_hbm, req_ref, w_hbm, out_ref,
    xin, win, xt, wt, reqm, r1, turned, rows, r2, idx, send, recv,
    xsem, wsem, lsem, s1, v1, s2, v2, dsend, drecv,
):
    atm = lax.axis_index("atm")
    ocn = lax.axis_index("ocn")
    xcopy = pltpu.make_async_copy(x_hbm, xin, xsem)
    xcopy.start()
    wcopy = pltpu.make_async_copy(w_hbm, win, wsem)
    wcopy.start()

    barrier = pltpu.get_barrier_semaphore()

    def greet_atm(i, carry):
        pl.semaphore_signal(barrier, inc=1, device_id=((atm + i) % NATM, ocn), device_id_type=MESH)
        return carry

    def greet_ocn(i, carry):
        pl.semaphore_signal(barrier, inc=1, device_id=(atm, (ocn + i) % NOCN), device_id_type=MESH)
        return carry

    lax.fori_loop(1, NATM, greet_atm, 0)
    lax.fori_loop(1, NOCN, greet_ocn, 0)

    for k in range(CAP):
        reqm[k : k + 1, :] = req_ref[k] & (NBLK - 1)
    reqm[CAP:, :] = jnp.zeros((KROWS - CAP, OWNERS), jnp.int32)

    pl.semaphore_wait(barrier, NATM + NOCN - 2)

    def first_hop(i, carry):
        pltpu.make_async_remote_copy(
            reqm, r1.at[atm], s1, v1, device_id=((atm + i) % NATM, ocn), device_id_type=MESH
        ).start()
        return carry

    lax.fori_loop(1, NATM, first_hop, 0)
    r1[atm] = reqm[...]

    xcopy.wait()
    xflat = xt.reshape(NBLK * HALF, 2 * CELLS)

    def turn_fields(tp, carry):
        both = jnp.concatenate([xin[tp], xin[tp + HALF]], axis=0).astype(jnp.float32)
        for b in range(0, NBLK, 128):
            xflat[pl.ds(b * HALF + tp, 128, stride=HALF), :] = jnp.transpose(both[:, b : b + 128])
        return carry

    lax.fori_loop(0, HALF // 2, turn_fields, 0)

    hop1 = pltpu.make_async_remote_copy(
        r1.at[pl.ds(0, NATM - 1)], r1.at[pl.ds(0, NATM - 1)], s1, v1,
        device_id=(atm, ocn), device_id_type=MESH,
    )
    hop1.wait_recv()
    half = r1[...].reshape(NATM * KROWS, OWNERS)
    turned[...] = jnp.transpose(jnp.concatenate([half, half], axis=0))
    mine = turned[pl.ds(pl.multiple_of(atm * NOCN, NOCN), NOCN), :]
    for o in range(NOCN):
        rows[o] = mine[o : o + 1, :]

    def second_hop(i, carry):
        to = (ocn + i) % NOCN
        pltpu.make_async_remote_copy(
            rows.at[to], r2.at[ocn], s2, v2, device_id=(atm, to), device_id_type=MESH
        ).start()
        return carry

    lax.fori_loop(1, NOCN, second_hop, 0)
    r2[ocn] = rows[ocn]

    lax.fori_loop(HALF // 2, HALF, turn_fields, 0)

    hop1.wait_send()
    hop2 = pltpu.make_async_remote_copy(
        r2.at[pl.ds(0, NOCN - 1)], r2.at[pl.ds(0, NOCN - 1)], s2, v2,
        device_id=(atm, ocn), device_id_type=MESH,
    )
    hop2.wait_recv()
    hop2.wait_send()
    tosmem = pltpu.make_async_copy(r2, idx, lsem)
    tosmem.start()
    tosmem.wait()

    left = lax.broadcasted_iota(jnp.int32, (HALF, 2 * CELLS), 1) < CELLS

    def fill(i, box, at):
        ta, to = moved(i, 1)
        for p in range(PAIRS):
            ia = idx[to, 0, ta * KROWS + 2 * p]
            ib = idx[to, 0, ta * KROWS + 2 * p + 1]
            a = xt[ia]
            b = xt[ib]
            low = jnp.where(left, a, pltpu.roll(b, CELLS, 1))
            high = jnp.where(left, pltpu.roll(a, CELLS, 1), b)
            box[at, p * TF : p * TF + HALF, :] = low.astype(jnp.bfloat16)
            box[at, p * TF + HALF : (p + 1) * TF, :] = high.astype(jnp.bfloat16)
        return ta, to

    fill(0, recv, 0)

    def ship(i, carry):
        ta, to = fill(i, send, i)
        pltpu.make_async_remote_copy(
            send.at[i], recv.at[i], dsend, drecv.at[i // PER],
            device_id=(ta, to), device_id_type=MESH,
        ).start()
        return carry

    for i in range(1, 4):
        ship(i, 0)

    def ship_four(q, carry):
        for i in range(4):
            ship(4 * q + i, 0)
        return carry

    lax.fori_loop(1, OWNERS // 4, ship_four, 0)

    wcopy.wait()
    for p in range(PAIRS):
        def turn_weights(a, carry):
            both = jnp.concatenate([win[2 * p, a], win[2 * p + 1, a]], axis=0).astype(jnp.float32)
            wt[p, pl.ds(a, OWNERS, stride=WPITCH), :] = jnp.transpose(both)
            return carry

        lax.fori_loop(0, CELLS, turn_weights, 0, unroll=8)

    lane = lax.broadcasted_iota(jnp.int32, (CELLS, 2 * CELLS), 1) < CELLS

    def apply(i, carry):
        fa, fo = moved(i, -1)
        s = fa * NOCN + fo
        for p in range(PAIRS):
            w = wt[p, pl.ds(pl.multiple_of(s * WPITCH, 8), CELLS), :]
            w = w.astype(jnp.bfloat16)
            zero = jnp.zeros_like(w)
            square = jnp.concatenate([jnp.where(lane, w, zero), jnp.where(lane, zero, w)], axis=0)
            part = jnp.dot(recv[i, p * TF : (p + 1) * TF, :], square, preferred_element_type=jnp.float32)
            out_ref[pl.ds(p * OWNERS + s, TF, stride=PAIRS * OWNERS), :] = part
        return carry

    for g in range(GROUPS):
        n = PER - 1 if g == 0 else PER
        pltpu.make_async_remote_copy(
            send.at[pl.ds(0, n)], recv.at[pl.ds(0, n)], dsend, drecv.at[g],
            device_id=(atm, ocn), device_id_type=MESH,
        ).wait_recv()
        lax.fori_loop(g * PER, (g + 1) * PER, apply, 0, unroll=4)

    pltpu.make_async_remote_copy(
        send.at[pl.ds(1, OWNERS - 1)], recv.at[pl.ds(1, OWNERS - 1)], dsend, drecv.at[0],
        device_id=(atm, ocn), device_id_type=MESH,
    ).wait_send()


def exchange(fields, req, mats):
    big = pl.BlockSpec(memory_space=pl.ANY)
    vmem = pl.BlockSpec(memory_space=pltpu.VMEM)
    return pl.pallas_call(
        exchange_kernel,
        out_shape=jax.ShapeDtypeStruct((TF * PAIRS * OWNERS, 2 * CELLS), jnp.float32),
        in_specs=[big, vmem, big],
        out_specs=vmem,
        scratch_shapes=[
            pltpu.VMEM((TF, CELLS, NBLK), jnp.bfloat16),
            pltpu.VMEM((CAP, CELLS, CELLS, OWNERS), jnp.bfloat16),
            pltpu.VMEM((NBLK, HALF, 2 * CELLS), jnp.float32),
            pltpu.VMEM((PAIRS, OWNERS * WPITCH, 2 * CELLS), jnp.float32),
            pltpu.VMEM((KROWS, OWNERS), jnp.int32),
            pltpu.VMEM((NATM, KROWS, OWNERS), jnp.int32),
            pltpu.VMEM((OWNERS, OWNERS), jnp.int32),
            pltpu.VMEM((NOCN, 1, OWNERS), jnp.int32),
            pltpu.VMEM((NOCN, 1, OWNERS), jnp.int32),
            pltpu.SMEM((NOCN, 1, OWNERS), jnp.int32),
            pltpu.VMEM((OWNERS, ROWS, 2 * CELLS), jnp.bfloat16),
            pltpu.VMEM((OWNERS, ROWS, 2 * CELLS), jnp.bfloat16),
            pltpu.SemaphoreType.DMA,
            pltpu.SemaphoreType.DMA,
            pltpu.SemaphoreType.DMA,
            pltpu.SemaphoreType.DMA,
            pltpu.SemaphoreType.DMA,
            pltpu.SemaphoreType.DMA,
            pltpu.SemaphoreType.DMA,
            pltpu.SemaphoreType.DMA,
            pltpu.SemaphoreType.DMA((GROUPS,)),
        ],
        compiler_params=pltpu.CompilerParams(
            collective_id=0, has_side_effects=True, vmem_limit_bytes=56 << 20
        ),
        name="exchange",
    )(fields, req, mats)


def place_kernel(p_ref, tgt_ref, cnt_ref, o_ref, hot, lhs):
    @pl.when(pl.program_id(0) == 0)
    def _():
        block = lax.broadcasted_iota(jnp.int32, (NBLK, OWNERS), 0)
        for par in range(2):
            for p in range(PAIRS):
                k = 2 * p + par
                live = jnp.where(cnt_ref[...] > k, tgt_ref[k], -1)
                at = (par * PAIRS + p) * OWNERS
                hot[:, at : at + OWNERS] = jnp.where(block == live, 1.0, 0.0).astype(jnp.bfloat16)

    nf = p_ref.shape[0]
    for f in range(nf):
        turned = jnp.transpose(p_ref[f])
        rows = jnp.concatenate([turned[:CELLS], turned[CELLS:]], axis=1)
        high = rows.astype(jnp.bfloat16)
        low = (rows - high.astype(jnp.float32)).astype(jnp.bfloat16)
        lhs[f * CELLS : (f + 1) * CELLS, :] = high
        lhs[(nf + f) * CELLS : (nf + f + 1) * CELLS, :] = low
    both = lax.dot_general(
        lhs[...], hot[...], (((1,), (1,)), ((), ())), preferred_element_type=jnp.float32
    )
    total = both[: nf * CELLS] + both[nf * CELLS :]
    o_ref[...] = total.reshape(nf, CELLS, NBLK)


def place(parts, targets, counts):
    nf = 8
    return pl.pallas_call(
        place_kernel,
        grid=(TF // nf,),
        out_shape=jax.ShapeDtypeStruct((TF, CELLS, NBLK), jnp.float32),
        in_specs=[
            pl.BlockSpec((nf, PAIRS * OWNERS, 2 * CELLS), lambda t: (t, 0, 0)),
            pl.BlockSpec((CAP, 1, OWNERS), lambda t: (0, 0, 0)),
            pl.BlockSpec((1, OWNERS), lambda t: (0, 0)),
        ],
        out_specs=pl.BlockSpec((nf, CELLS, NBLK), lambda t: (t, 0, 0)),
        scratch_shapes=[
            pltpu.VMEM((NBLK, 2 * PAIRS * OWNERS), jnp.bfloat16),
            pltpu.VMEM((2 * nf * CELLS, 2 * PAIRS * OWNERS), jnp.bfloat16),
        ],
        compiler_params=pltpu.CompilerParams(vmem_limit_bytes=48 << 20),
        name="place",
    )(parts, targets, counts)


def on_device(atm_fields, requests, ocean_block, live_counts, weights):
    fields = jnp.transpose(atm_fields, (1, 2, 3, 0)).reshape(TF, CELLS, NBLK)
    req = jnp.transpose(requests, (2, 0, 1))
    targets = jnp.transpose(ocean_block, (2, 0, 1))
    mats = jnp.transpose(weights[0], (1, 2, 3, 0))
    parts = exchange(fields, req, mats)
    out = place(parts.reshape(TF, PAIRS * OWNERS, 2 * CELLS), targets, live_counts)
    return jnp.transpose(out.reshape(4, 8, CELLS, NBLK), (3, 0, 1, 2))


def solution(mesh):
    in_specs = (
        P(("atm", "ocn"), None, None, None),
        P(("atm", "ocn"), None, None),
        P(("atm", "ocn"), None, None),
        P(("atm", "ocn"), None),
        P(("atm", "ocn"), None, None, None, None),
    )
    out_specs = P(("atm", "ocn"), None, None, None)
    return jax.shard_map(
        on_device, mesh=mesh, in_specs=in_specs, out_specs=out_specs, check_vma=False
    )
```

```python
import jax
import jax.numpy as jnp
from jax import lax
from jax.experimental import pallas as pl
from jax.experimental.pallas import tpu as pltpu
from jax.sharding import PartitionSpec as P

MESH = pl.DeviceIdType.MESH
OWNERS = 128
NATM = 8
NOCN = 16
CAP = 6
KROWS = 8
PAIRS = 3
CELLS = 64
TF = 32
HALF = 16
NBLK = 512
GROUPS = 16
TFS = 16
PER = OWNERS // GROUPS
ROWS = PAIRS * TF
WPITCH = CELLS


def shift_of(i):
    j = (i * 37) % OWNERS
    return j // 32, (j // 16) % 2, (j // 4) % 4, j % 4


def moved(i, sign):
    atm = lax.axis_index("atm")
    ocn = lax.axis_index("ocn")
    dy, dc, dx, dz = shift_of(i)
    y = (atm // 2 + 4 + sign * dy) % 4
    c = (atm % 2 + 2 + sign * dc) % 2
    x = (ocn // 4 + 4 + sign * dx) % 4
    z = (ocn % 4 + 4 + sign * dz) % 4
    return y * 2 + c, x * 4 + z


def sender_of(i):
    atm = lax.axis_index("atm")
    ocn = lax.axis_index("ocn")
    j = (i * 37) & (OWNERS - 1)
    y = (atm // 2 - (j >> 5)) & 3
    c = (atm % 2 - (j >> 4)) & 1
    x = (ocn // 4 - (j >> 2)) & 3
    z = (ocn % 4 - j) & 3
    return ((y * 2 + c) * 4 + x) * 4 + z


def exchange_kernel(
    x_hbm, req_hbm, w_hbm, tgt_hbm, cnt_hbm, acc,
    req_ref, tgt_ref, cnt_ref, xin, win, xt, wt, reqm, r1, turned, rows, r2, idx, send, recv, part, lhs, hot,
    xsem, wsem, lsem, isem, s1, v1, s2, v2, dsend, drecv,
):
    atm = lax.axis_index("atm")
    ocn = lax.axis_index("ocn")
    small = [
        pltpu.make_async_copy(a, b, isem.at[n])
        for n, (a, b) in enumerate(((req_hbm, req_ref), (tgt_hbm, tgt_ref), (cnt_hbm, cnt_ref)))
    ]
    for copy in small:
        copy.start()
    xcopy = pltpu.make_async_copy(x_hbm, xin, xsem)
    xcopy.start()
    wcopy = pltpu.make_async_copy(w_hbm, win, wsem)
    wcopy.start()

    barrier = pltpu.get_barrier_semaphore()

    for i in range(1, NATM):
        pl.semaphore_signal(barrier, inc=1, device_id=((atm + i) % NATM, ocn), device_id_type=MESH)
    for i in range(1, NOCN):
        pl.semaphore_signal(barrier, inc=1, device_id=(atm, (ocn + i) % NOCN), device_id_type=MESH)
    small[0].wait()
    for k in range(CAP):
        reqm[k : k + 1, :] = req_ref[k] & (NBLK - 1)
    reqm[CAP:, :] = jnp.zeros((KROWS - CAP, OWNERS), jnp.int32)

    pl.semaphore_wait(barrier, NATM + NOCN - 2)

    for i in range(1, NATM):
        pltpu.make_async_remote_copy(
            reqm, r1.at[atm], s1, v1, device_id=((atm + i) % NATM, ocn), device_id_type=MESH
        ).start()
    r1[atm] = reqm[...]

    xcopy.wait()
    xflat = xt.reshape(NBLK * HALF, 2 * CELLS)

    def turn_fields(tp, carry):
        both = jnp.concatenate([xin[tp], xin[tp + HALF]], axis=0).astype(jnp.float32)
        for b in range(0, NBLK, 128):
            xflat[pl.ds(b * HALF + tp, 128, stride=HALF), :] = jnp.transpose(both[:, b : b + 128])
        return carry

    lax.fori_loop(0, HALF // 2, turn_fields, 0)

    hop1 = pltpu.make_async_remote_copy(
        r1.at[pl.ds(0, NATM - 1)], r1.at[pl.ds(0, NATM - 1)], s1, v1,
        device_id=(atm, ocn), device_id_type=MESH,
    )
    hop1.wait_recv()
    half = r1[...].reshape(NATM * KROWS, OWNERS)
    turned[...] = jnp.transpose(jnp.concatenate([half, half], axis=0))
    mine = turned[pl.ds(pl.multiple_of(atm * NOCN, NOCN), NOCN), :]
    for o in range(NOCN):
        rows[o] = mine[o : o + 1, :]

    for i in range(1, NOCN):
        to = (ocn + i) % NOCN
        pltpu.make_async_remote_copy(
            rows.at[to], r2.at[ocn], s2, v2, device_id=(atm, to), device_id_type=MESH
        ).start()
    r2[ocn] = rows[ocn]

    lax.fori_loop(HALF // 2, HALF, turn_fields, 0)

    hop1.wait_send()
    hop2 = pltpu.make_async_remote_copy(
        r2.at[pl.ds(0, NOCN - 1)], r2.at[pl.ds(0, NOCN - 1)], s2, v2,
        device_id=(atm, ocn), device_id_type=MESH,
    )
    hop2.wait_recv()
    hop2.wait_send()
    tosmem = pltpu.make_async_copy(r2, idx, lsem)
    tosmem.start()
    tosmem.wait()

    left = lax.broadcasted_iota(jnp.int32, (HALF, 2 * CELLS), 1) < CELLS

    def fill(i, box, at):
        ta, to = moved(i, 1)
        for p in range(PAIRS):
            ia = idx[to, 0, ta * KROWS + 2 * p]
            ib = idx[to, 0, ta * KROWS + 2 * p + 1]
            a = xt[ia]
            b = xt[ib]
            low = jnp.where(left, a, pltpu.roll(b, CELLS, 1))
            high = jnp.where(left, pltpu.roll(a, CELLS, 1), b)
            box[at, p * TF : p * TF + HALF, :] = low.astype(jnp.bfloat16)
            box[at, p * TF + HALF : (p + 1) * TF, :] = high.astype(jnp.bfloat16)
        return ta, to

    fill(0, recv, 0)

    def ship(i, carry):
        ta, to = fill(i, send, i)
        pltpu.make_async_remote_copy(
            send.at[i], recv.at[i], dsend, drecv.at[i // PER],
            device_id=(ta, to), device_id_type=MESH,
        ).start()
        return carry

    for i in range(1, 4):
        ship(i, 0)

    def ship_four(q, carry):
        for i in range(4):
            ship(4 * q + i, 0)
        return carry

    lax.fori_loop(1, OWNERS // 4, ship_four, 0)

    wcopy.wait()
    for p in range(PAIRS):
        def turn_weights(a, carry):
            both = jnp.concatenate([win[2 * p, a], win[2 * p + 1, a]], axis=0).astype(jnp.float32)
            wt[p, pl.ds(a, OWNERS, stride=WPITCH), :] = jnp.transpose(both)
            return carry

        lax.fori_loop(0, CELLS, turn_weights, 0, unroll=8)

    small[1].wait()
    small[2].wait()
    j = lax.broadcasted_iota(jnp.int32, (PAIRS * OWNERS, OWNERS), 0)
    step = (j * 171) >> 9
    pair = j - PAIRS * step
    came = sender_of(step)
    col = lax.broadcasted_iota(jnp.int32, (PAIRS * OWNERS, OWNERS), 1)
    found = jnp.zeros((PAIRS * OWNERS, KROWS), jnp.float32)
    for p in range(PAIRS):
        pick = jnp.where((came == col) & (pair == p), 1.0, 0.0).astype(jnp.bfloat16)
        terms = []
        for par in range(2):
            k = 2 * p + par
            goal = jnp.where(cnt_ref[...] > k, tgt_ref[k] + 1, 0)
            terms += [goal >> 4, goal & 15]
        terms = jnp.concatenate(terms + terms, axis=0).astype(jnp.float32).astype(jnp.bfloat16)
        found += lax.dot_general(
            pick, terms, (((1,), (1,)), ((), ())), preferred_element_type=jnp.float32
        )
    block = lax.broadcasted_iota(jnp.int32, (OWNERS, NBLK), 1).astype(jnp.float32)
    for par in range(2):
        goal = found[:, 2 * par : 2 * par + 1] * 16.0 + found[:, 2 * par + 1 : 2 * par + 2] - 1.0
        for b in range(PAIRS):
            mine = goal[b * OWNERS : (b + 1) * OWNERS]
            ones = jnp.where(block == mine, 1.0, 0.0).astype(jnp.bfloat16)
            for h in range(2):
                at = (2 * h + par) * OWNERS
                hot[b, at : at + OWNERS, :] = ones

    lane = lax.broadcasted_iota(jnp.int32, (CELLS, 2 * CELLS), 1) < CELLS

    def apply(i, carry):
        fa, fo = moved(i, -1)
        s = fa * NOCN + fo
        for p in range(PAIRS):
            w = wt[p, pl.ds(pl.multiple_of(s * WPITCH, 8), CELLS), :]
            w = w.astype(jnp.bfloat16)
            zero = jnp.zeros_like(w)
            square = jnp.concatenate([jnp.where(lane, w, zero), jnp.where(lane, zero, w)], axis=0)
            prod = jnp.dot(recv[i, p * TF : (p + 1) * TF, :], square, preferred_element_type=jnp.float32)
            part[pl.ds(PAIRS * i + p, TF, stride=PAIRS * OWNERS), :] = prod
        return carry

    def turn_parts(b, tf):
        rows = part[pl.ds(pl.multiple_of(tf * PAIRS * OWNERS + b * OWNERS, OWNERS), OWNERS), :]
        rows = jnp.transpose(rows)
        high = rows.astype(jnp.bfloat16)
        low = (rows - high.astype(jnp.float32)).astype(jnp.bfloat16)
        at = pl.ds(pl.multiple_of(tf * CELLS, CELLS), CELLS)
        for h, term in enumerate((high, low)):
            lhs[at, 2 * h * OWNERS : (2 * h + 1) * OWNERS] = term[:CELLS]
            lhs[at, (2 * h + 1) * OWNERS : (2 * h + 2) * OWNERS] = term[CELLS:]

    def place(b, tf):
        at = pl.ds(pl.multiple_of(tf * CELLS, CELLS), TFS * CELLS)
        more = jnp.dot(lhs[at, :], hot[b], preferred_element_type=jnp.float32)
        if b:
            more += acc[at, :]
        acc[at, :] = more

    for g in range(GROUPS):
        n = PER - 1 if g == 0 else PER
        pltpu.make_async_remote_copy(
            send.at[pl.ds(0, n)], recv.at[pl.ds(0, n)], dsend, drecv.at[g],
            device_id=(atm, ocn), device_id_type=MESH,
        ).wait_recv()
        lax.fori_loop(g * PER, (g + 1) * PER, apply, 0, unroll=4)
        for b in range(PAIRS):
            if g * PER * PAIRS < (b + 1) * OWNERS <= (g + 1) * PER * PAIRS:
                def some(q, carry):
                    for t in range(TFS):
                        turn_parts(b, q * TFS + t)
                    place(b, q * TFS)
                    return carry

                lax.fori_loop(0, TF // TFS, some, 0)

    pltpu.make_async_remote_copy(
        send.at[pl.ds(1, OWNERS - 1)], recv.at[pl.ds(1, OWNERS - 1)], dsend, drecv.at[0],
        device_id=(atm, ocn), device_id_type=MESH,
    ).wait_send()


def exchange(fields, req, mats, targets, counts):
    far = pl.BlockSpec(memory_space=pltpu.HBM)
    return pl.pallas_call(
        exchange_kernel,
        out_shape=pltpu.VMEM((TF * CELLS, NBLK), jnp.float32),
        in_specs=[far] * 5,
        out_specs=pl.BlockSpec(memory_space=pltpu.VMEM),
        scratch_shapes=[
            pltpu.VMEM((CAP, 1, OWNERS), jnp.int32),
            pltpu.VMEM((CAP, 1, OWNERS), jnp.int32),
            pltpu.VMEM((1, OWNERS), jnp.int32),
            pltpu.VMEM((TF, CELLS, NBLK), jnp.bfloat16),
            pltpu.VMEM((CAP, CELLS, CELLS, OWNERS), jnp.bfloat16),
            pltpu.VMEM((NBLK, HALF, 2 * CELLS), jnp.float32),
            pltpu.VMEM((PAIRS, OWNERS * WPITCH, 2 * CELLS), jnp.float32),
            pltpu.VMEM((KROWS, OWNERS), jnp.int32),
            pltpu.VMEM((NATM, KROWS, OWNERS), jnp.int32),
            pltpu.VMEM((OWNERS, OWNERS), jnp.int32),
            pltpu.VMEM((NOCN, 1, OWNERS), jnp.int32),
            pltpu.VMEM((NOCN, 1, OWNERS), jnp.int32),
            pltpu.SMEM((NOCN, 1, OWNERS), jnp.int32),
            pltpu.VMEM((OWNERS, ROWS, 2 * CELLS), jnp.bfloat16),
            pltpu.VMEM((OWNERS, ROWS, 2 * CELLS), jnp.bfloat16),
            pltpu.VMEM((TF * PAIRS * OWNERS, 2 * CELLS), jnp.float32),
            pltpu.VMEM((TF * CELLS, 4 * OWNERS), jnp.bfloat16),
            pltpu.VMEM((PAIRS, 4 * OWNERS, NBLK), jnp.bfloat16),
            pltpu.SemaphoreType.DMA,
            pltpu.SemaphoreType.DMA,
            pltpu.SemaphoreType.DMA,
            pltpu.SemaphoreType.DMA((3,)),
            pltpu.SemaphoreType.DMA,
            pltpu.SemaphoreType.DMA,
            pltpu.SemaphoreType.DMA,
            pltpu.SemaphoreType.DMA,
            pltpu.SemaphoreType.DMA,
            pltpu.SemaphoreType.DMA((GROUPS,)),
        ],
        compiler_params=pltpu.CompilerParams(
            collective_id=0, has_side_effects=True, vmem_limit_bytes=56 << 20
        ),
        name="exchange",
    )(fields, req, mats, targets, counts)


def on_device(atm_fields, requests, ocean_block, live_counts, weights):
    fields = jnp.transpose(atm_fields, (1, 2, 3, 0)).reshape(TF, CELLS, NBLK)
    req = jnp.transpose(requests, (2, 0, 1))
    targets = jnp.transpose(ocean_block, (2, 0, 1))
    mats = jnp.transpose(weights[0], (1, 2, 3, 0))
    out = exchange(fields, req, mats, targets, live_counts)
    return jnp.transpose(out.reshape(4, 8, CELLS, NBLK), (3, 0, 1, 2))


def solution(mesh):
    in_specs = (
        P(("atm", "ocn"), None, None, None),
        P(("atm", "ocn"), None, None),
        P(("atm", "ocn"), None, None),
        P(("atm", "ocn"), None),
        P(("atm", "ocn"), None, None, None, None),
    )
    out_specs = P(("atm", "ocn"), None, None, None)
    return jax.shard_map(
        on_device, mesh=mesh, in_specs=in_specs, out_specs=out_specs, check_vma=False
    )
```

```python
import jax
import jax.numpy as jnp
from jax import lax
from jax.experimental import pallas as pl
from jax.experimental.pallas import tpu as pltpu
from jax.sharding import PartitionSpec as P

MESH = pl.DeviceIdType.MESH
OWNERS = 128
NATM = 8
NOCN = 16
CAP = 6
KROWS = 8
PAIRS = 3
CELLS = 64
TF = 32
HALF = 16
NBLK = 512
GROUPS = 16
TFS = 32
PER = OWNERS // GROUPS
ROWS = PAIRS * TF
WPITCH = CELLS


def shift_of(i):
    j = (i * 59) % OWNERS
    return j // 32, (j // 16) % 2, (j // 4) % 4, j % 4


def moved(i, sign):
    atm = lax.axis_index("atm")
    ocn = lax.axis_index("ocn")
    dy, dc, dx, dz = shift_of(i)
    y = (atm // 2 + 4 + sign * dy) % 4
    c = (atm % 2 + 2 + sign * dc) % 2
    x = (ocn // 4 + 4 + sign * dx) % 4
    z = (ocn % 4 + 4 + sign * dz) % 4
    return y * 2 + c, x * 4 + z


def sender_of(i):
    atm = lax.axis_index("atm")
    ocn = lax.axis_index("ocn")
    j = (i * 59) & (OWNERS - 1)
    y = (atm // 2 - (j >> 5)) & 3
    c = (atm % 2 - (j >> 4)) & 1
    x = (ocn // 4 - (j >> 2)) & 3
    z = (ocn % 4 - j) & 3
    return ((y * 2 + c) * 4 + x) * 4 + z


def exchange_kernel(
    x_hbm, req_hbm, w_hbm, tgt_hbm, cnt_hbm, acc,
    req_ref, tgt_ref, cnt_ref, xin, win, xt, wt, reqm, r1, turned, rows, r2, idx, send, recv, part, lhs, hot,
    xsem, wsem, lsem, isem, s1, v1, s2, v2, dsend, drecv,
):
    atm = lax.axis_index("atm")
    ocn = lax.axis_index("ocn")
    small = [
        pltpu.make_async_copy(a, b, isem.at[n])
        for n, (a, b) in enumerate(((req_hbm, req_ref), (tgt_hbm, tgt_ref), (cnt_hbm, cnt_ref)))
    ]
    for copy in small:
        copy.start()
    xcopy = pltpu.make_async_copy(x_hbm, xin, xsem)
    xcopy.start()
    wcopy = pltpu.make_async_copy(w_hbm, win, wsem)
    wcopy.start()

    barrier = pltpu.get_barrier_semaphore()

    for i in range(1, NATM):
        pl.semaphore_signal(barrier, inc=1, device_id=((atm + i) % NATM, ocn), device_id_type=MESH)
    for i in range(1, NOCN):
        pl.semaphore_signal(barrier, inc=1, device_id=(atm, (ocn + i) % NOCN), device_id_type=MESH)
    small[0].wait()
    for k in range(CAP):
        reqm[k : k + 1, :] = req_ref[k] & (NBLK - 1)
    reqm[CAP:, :] = jnp.zeros((KROWS - CAP, OWNERS), jnp.int32)

    pl.semaphore_wait(barrier, NATM + NOCN - 2)

    for i in range(1, NATM):
        pltpu.make_async_remote_copy(
            reqm, r1.at[atm], s1, v1, device_id=((atm + i) % NATM, ocn), device_id_type=MESH
        ).start()
    r1[atm] = reqm[...]

    xcopy.wait()
    xflat = xt.reshape(NBLK * HALF, 2 * CELLS)

    def turn_fields(tp, carry):
        both = jnp.concatenate([xin[tp], xin[tp + HALF]], axis=0).astype(jnp.float32)
        for b in range(0, NBLK, 128):
            xflat[pl.ds(b * HALF + tp, 128, stride=HALF), :] = jnp.transpose(both[:, b : b + 128])
        return carry

    lax.fori_loop(0, HALF // 2, turn_fields, 0)

    hop1 = pltpu.make_async_remote_copy(
        r1.at[pl.ds(0, NATM - 1)], r1.at[pl.ds(0, NATM - 1)], s1, v1,
        device_id=(atm, ocn), device_id_type=MESH,
    )
    hop1.wait_recv()
    half = r1[...].reshape(NATM * KROWS, OWNERS)
    turned[...] = jnp.transpose(jnp.concatenate([half, half], axis=0))
    mine = turned[pl.ds(pl.multiple_of(atm * NOCN, NOCN), NOCN), :]
    for o in range(NOCN):
        rows[o] = mine[o : o + 1, :]

    for i in range(1, NOCN):
        to = (ocn + i) % NOCN
        pltpu.make_async_remote_copy(
            rows.at[to], r2.at[ocn], s2, v2, device_id=(atm, to), device_id_type=MESH
        ).start()
    r2[ocn] = rows[ocn]

    lax.fori_loop(HALF // 2, HALF, turn_fields, 0)

    hop1.wait_send()
    hop2 = pltpu.make_async_remote_copy(
        r2.at[pl.ds(0, NOCN - 1)], r2.at[pl.ds(0, NOCN - 1)], s2, v2,
        device_id=(atm, ocn), device_id_type=MESH,
    )
    hop2.wait_recv()
    hop2.wait_send()
    tosmem = pltpu.make_async_copy(r2, idx, lsem)
    tosmem.start()
    tosmem.wait()

    left = lax.broadcasted_iota(jnp.int32, (HALF, 2 * CELLS), 1) < CELLS

    def fill(i, box, at):
        ta, to = moved(i, 1)
        for p in range(PAIRS):
            ia = idx[to, 0, ta * KROWS + 2 * p]
            ib = idx[to, 0, ta * KROWS + 2 * p + 1]
            a = xt[ia]
            b = xt[ib]
            low = jnp.where(left, a, pltpu.roll(b, CELLS, 1))
            high = jnp.where(left, pltpu.roll(a, CELLS, 1), b)
            box[at, p * TF : p * TF + HALF, :] = low.astype(jnp.bfloat16)
            box[at, p * TF + HALF : (p + 1) * TF, :] = high.astype(jnp.bfloat16)
        return ta, to

    fill(0, recv, 0)

    def ship(i, carry):
        ta, to = fill(i, send, i)
        pltpu.make_async_remote_copy(
            send.at[i], recv.at[i], dsend, drecv.at[i // PER],
            device_id=(ta, to), device_id_type=MESH,
        ).start()
        return carry

    for i in range(1, 4):
        ship(i, 0)

    def ship_four(q, carry):
        for i in range(4):
            ship(4 * q + i, 0)
        return carry

    lax.fori_loop(1, OWNERS // 4, ship_four, 0)

    wcopy.wait()
    for p in range(PAIRS):
        def turn_weights(a, carry):
            both = jnp.concatenate([win[2 * p, a], win[2 * p + 1, a]], axis=0).astype(jnp.float32)
            wt[p, pl.ds(a, OWNERS, stride=WPITCH), :] = jnp.transpose(both)
            return carry

        lax.fori_loop(0, CELLS, turn_weights, 0, unroll=8)

    small[1].wait()
    small[2].wait()
    j = lax.broadcasted_iota(jnp.int32, (PAIRS * OWNERS, OWNERS), 0)
    step = (j * 171) >> 9
    pair = j - PAIRS * step
    came = sender_of(step)
    col = lax.broadcasted_iota(jnp.int32, (PAIRS * OWNERS, OWNERS), 1)
    found = jnp.zeros((PAIRS * OWNERS, KROWS), jnp.float32)
    for p in range(PAIRS):
        pick = jnp.where((came == col) & (pair == p), 1.0, 0.0).astype(jnp.bfloat16)
        terms = []
        for par in range(2):
            k = 2 * p + par
            goal = jnp.where(cnt_ref[...] > k, tgt_ref[k] + 1, 0)
            terms += [goal >> 4, goal & 15]
        terms = jnp.concatenate(terms + terms, axis=0).astype(jnp.float32).astype(jnp.bfloat16)
        found += lax.dot_general(
            pick, terms, (((1,), (1,)), ((), ())), preferred_element_type=jnp.float32
        )
    block = lax.broadcasted_iota(jnp.int32, (OWNERS, NBLK), 1).astype(jnp.float32)
    for par in range(2):
        goal = found[:, 2 * par : 2 * par + 1] * 16.0 + found[:, 2 * par + 1 : 2 * par + 2] - 1.0
        for b in range(PAIRS):
            mine = goal[b * OWNERS : (b + 1) * OWNERS]
            ones = jnp.where(block == mine, 1.0, 0.0).astype(jnp.bfloat16)
            for h in range(2):
                at = (2 * h + par) * OWNERS
                hot[b, at : at + OWNERS, :] = ones

    lane = lax.broadcasted_iota(jnp.int32, (CELLS, 2 * CELLS), 1) < CELLS

    def apply(i, carry):
        fa, fo = moved(i, -1)
        s = fa * NOCN + fo
        for p in range(PAIRS):
            w = wt[p, pl.ds(pl.multiple_of(s * WPITCH, 8), CELLS), :]
            w = w.astype(jnp.bfloat16)
            zero = jnp.zeros_like(w)
            square = jnp.concatenate([jnp.where(lane, w, zero), jnp.where(lane, zero, w)], axis=0)
            prod = jnp.dot(recv[i, p * TF : (p + 1) * TF, :], square, preferred_element_type=jnp.float32)
            part[pl.ds(PAIRS * i + p, TF, stride=PAIRS * OWNERS), :] = prod
        return carry

    def turn_parts(b, tf):
        rows = part[pl.ds(pl.multiple_of(tf * PAIRS * OWNERS + b * OWNERS, OWNERS), OWNERS), :]
        rows = jnp.transpose(rows)
        high = rows.astype(jnp.bfloat16)
        low = (rows - high.astype(jnp.float32)).astype(jnp.bfloat16)
        at = pl.ds(pl.multiple_of(tf * CELLS, CELLS), CELLS)
        for h, term in enumerate((high, low)):
            lhs[at, 2 * h * OWNERS : (2 * h + 1) * OWNERS] = term[:CELLS]
            lhs[at, (2 * h + 1) * OWNERS : (2 * h + 2) * OWNERS] = term[CELLS:]

    def place(b, tf):
        at = pl.ds(pl.multiple_of(tf * CELLS, CELLS), TFS * CELLS)
        more = jnp.dot(lhs[at, :], hot[b], preferred_element_type=jnp.float32)
        if b:
            more += acc[at, :]
        acc[at, :] = more

    for g in range(GROUPS):
        n = PER - 1 if g == 0 else PER
        pltpu.make_async_remote_copy(
            send.at[pl.ds(0, n)], recv.at[pl.ds(0, n)], dsend, drecv.at[g],
            device_id=(atm, ocn), device_id_type=MESH,
        ).wait_recv()
        lax.fori_loop(g * PER, (g + 1) * PER, apply, 0, unroll=8)
        for b in range(PAIRS):
            if g * PER * PAIRS < (b + 1) * OWNERS <= (g + 1) * PER * PAIRS:
                def some(q, carry):
                    for t in range(TFS):
                        turn_parts(b, q * TFS + t)
                    place(b, q * TFS)
                    return carry

                lax.fori_loop(0, TF // TFS, some, 0)

    pltpu.make_async_remote_copy(
        send.at[pl.ds(1, OWNERS - 1)], recv.at[pl.ds(1, OWNERS - 1)], dsend, drecv.at[0],
        device_id=(atm, ocn), device_id_type=MESH,
    ).wait_send()


def exchange(fields, req, mats, targets, counts):
    far = pl.BlockSpec(memory_space=pltpu.HBM)
    return pl.pallas_call(
        exchange_kernel,
        out_shape=pltpu.VMEM((TF * CELLS, NBLK), jnp.float32),
        in_specs=[far] * 5,
        out_specs=pl.BlockSpec(memory_space=pltpu.VMEM),
        scratch_shapes=[
            pltpu.VMEM((CAP, 1, OWNERS), jnp.int32),
            pltpu.VMEM((CAP, 1, OWNERS), jnp.int32),
            pltpu.VMEM((1, OWNERS), jnp.int32),
            pltpu.VMEM((TF, CELLS, NBLK), jnp.bfloat16),
            pltpu.VMEM((CAP, CELLS, CELLS, OWNERS), jnp.bfloat16),
            pltpu.VMEM((NBLK, HALF, 2 * CELLS), jnp.float32),
            pltpu.VMEM((PAIRS, OWNERS * WPITCH, 2 * CELLS), jnp.float32),
            pltpu.VMEM((KROWS, OWNERS), jnp.int32),
            pltpu.VMEM((NATM, KROWS, OWNERS), jnp.int32),
            pltpu.VMEM((OWNERS, OWNERS), jnp.int32),
            pltpu.VMEM((NOCN, 1, OWNERS), jnp.int32),
            pltpu.VMEM((NOCN, 1, OWNERS), jnp.int32),
            pltpu.SMEM((NOCN, 1, OWNERS), jnp.int32),
            pltpu.VMEM((OWNERS, ROWS, 2 * CELLS), jnp.bfloat16),
            pltpu.VMEM((OWNERS, ROWS, 2 * CELLS), jnp.bfloat16),
            pltpu.VMEM((TF * PAIRS * OWNERS, 2 * CELLS), jnp.float32),
            pltpu.VMEM((TF * CELLS, 4 * OWNERS), jnp.bfloat16),
            pltpu.VMEM((PAIRS, 4 * OWNERS, NBLK), jnp.bfloat16),
            pltpu.SemaphoreType.DMA,
            pltpu.SemaphoreType.DMA,
            pltpu.SemaphoreType.DMA,
            pltpu.SemaphoreType.DMA((3,)),
            pltpu.SemaphoreType.DMA,
            pltpu.SemaphoreType.DMA,
            pltpu.SemaphoreType.DMA,
            pltpu.SemaphoreType.DMA,
            pltpu.SemaphoreType.DMA,
            pltpu.SemaphoreType.DMA((GROUPS,)),
        ],
        compiler_params=pltpu.CompilerParams(
            collective_id=0, has_side_effects=True, vmem_limit_bytes=56 << 20
        ),
        name="exchange",
    )(fields, req, mats, targets, counts)


def on_device(atm_fields, requests, ocean_block, live_counts, weights):
    fields = jnp.transpose(atm_fields, (1, 2, 3, 0)).reshape(TF, CELLS, NBLK)
    req = jnp.transpose(requests, (2, 0, 1))
    targets = jnp.transpose(ocean_block, (2, 0, 1))
    mats = jnp.transpose(weights[0], (1, 2, 3, 0))
    out = exchange(fields, req, mats, targets, live_counts)
    return jnp.transpose(out.reshape(4, 8, CELLS, NBLK), (3, 0, 1, 2))


def solution(mesh):
    in_specs = (
        P(("atm", "ocn"), None, None, None),
        P(("atm", "ocn"), None, None),
        P(("atm", "ocn"), None, None),
        P(("atm", "ocn"), None),
        P(("atm", "ocn"), None, None, None, None),
    )
    out_specs = P(("atm", "ocn"), None, None, None)
    return jax.shard_map(
        on_device, mesh=mesh, in_specs=in_specs, out_specs=out_specs, check_vma=False
    )
```

```python
import jax
import jax.numpy as jnp
from jax import lax
from jax.experimental import pallas as pl
from jax.experimental.pallas import tpu as pltpu
from jax.sharding import PartitionSpec as P

MESH = pl.DeviceIdType.MESH
OWNERS = 128
NATM = 8
NOCN = 16
CAP = 6
KROWS = 8
PAIRS = 3
CELLS = 64
TF = 32
HALF = 16
NBLK = 512
GROUPS = 16
PER = OWNERS // GROUPS
ROWS = PAIRS * TF
WPITCH = CELLS


def shift_of(i):
    j = (i * 91) % OWNERS
    return j // 32, (j // 16) % 2, (j // 4) % 4, j % 4


def moved(i, sign):
    atm = lax.axis_index("atm")
    ocn = lax.axis_index("ocn")
    dy, dc, dx, dz = shift_of(i)
    y = (atm // 2 + 4 + sign * dy) % 4
    c = (atm % 2 + 2 + sign * dc) % 2
    x = (ocn // 4 + 4 + sign * dx) % 4
    z = (ocn % 4 + 4 + sign * dz) % 4
    return y * 2 + c, x * 4 + z


def sender_of(i):
    atm = lax.axis_index("atm")
    ocn = lax.axis_index("ocn")
    j = (i * 91) & (OWNERS - 1)
    y = (atm // 2 - (j >> 5)) & 3
    c = (atm % 2 - (j >> 4)) & 1
    x = (ocn // 4 - (j >> 2)) & 3
    z = (ocn % 4 - j) & 3
    return ((y * 2 + c) * 4 + x) * 4 + z


def exchange_kernel(
    x_hbm, req_hbm, w_hbm, tgt_hbm, cnt_hbm, acc,
    req_ref, tgt_ref, cnt_ref, xin, win, xt, wt, reqm, r1, turned, rows, r2, idx, send, recv, part, lhs, hot,
    xsem, wsem, lsem, isem, s1, v1, s2, v2, dsend, drecv,
):
    atm = lax.axis_index("atm")
    ocn = lax.axis_index("ocn")
    small = [
        pltpu.make_async_copy(a, b, isem.at[n])
        for n, (a, b) in enumerate(((req_hbm, req_ref), (tgt_hbm, tgt_ref), (cnt_hbm, cnt_ref)))
    ]
    for copy in small:
        copy.start()
    xcopy = pltpu.make_async_copy(x_hbm, xin, xsem)
    xcopy.start()
    wcopy = pltpu.make_async_copy(w_hbm, win, wsem)
    wcopy.start()

    barrier = pltpu.get_barrier_semaphore()

    for i in range(1, NATM):
        pl.semaphore_signal(barrier, inc=1, device_id=((atm + i) % NATM, ocn), device_id_type=MESH)
    for i in range(1, NOCN):
        pl.semaphore_signal(barrier, inc=1, device_id=(atm, (ocn + i) % NOCN), device_id_type=MESH)
    small[0].wait()
    for k in range(CAP):
        reqm[k : k + 1, :] = req_ref[k] & (NBLK - 1)
    reqm[CAP:, :] = jnp.zeros((KROWS - CAP, OWNERS), jnp.int32)

    pl.semaphore_wait(barrier, NATM + NOCN - 2)

    for i in range(1, NATM):
        pltpu.make_async_remote_copy(
            reqm, r1.at[atm], s1, v1, device_id=((atm + i) % NATM, ocn), device_id_type=MESH
        ).start()
    r1[atm] = reqm[...]

    xcopy.wait()
    xflat = xt.reshape(NBLK * HALF, 2 * CELLS)

    def turn_fields(tp, carry):
        both = jnp.concatenate([xin[tp], xin[tp + HALF]], axis=0).astype(jnp.float32)
        for b in range(0, NBLK, 128):
            xflat[pl.ds(b * HALF + tp, 128, stride=HALF), :] = jnp.transpose(both[:, b : b + 128])
        return carry

    lax.fori_loop(0, HALF // 2, turn_fields, 0)

    hop1 = pltpu.make_async_remote_copy(
        r1.at[pl.ds(0, NATM - 1)], r1.at[pl.ds(0, NATM - 1)], s1, v1,
        device_id=(atm, ocn), device_id_type=MESH,
    )
    hop1.wait_recv()
    half = r1[...].reshape(NATM * KROWS, OWNERS)
    turned[...] = jnp.transpose(jnp.concatenate([half, half], axis=0))
    mine = turned[pl.ds(pl.multiple_of(atm * NOCN, NOCN), NOCN), :]
    for o in range(NOCN):
        rows[o] = mine[o : o + 1, :]

    for i in range(1, NOCN):
        to = (ocn + i) % NOCN
        pltpu.make_async_remote_copy(
            rows.at[to], r2.at[ocn], s2, v2, device_id=(atm, to), device_id_type=MESH
        ).start()
    r2[ocn] = rows[ocn]

    lax.fori_loop(HALF // 2, HALF, turn_fields, 0)

    hop1.wait_send()
    hop2 = pltpu.make_async_remote_copy(
        r2.at[pl.ds(0, NOCN - 1)], r2.at[pl.ds(0, NOCN - 1)], s2, v2,
        device_id=(atm, ocn), device_id_type=MESH,
    )
    hop2.wait_recv()
    hop2.wait_send()
    tosmem = pltpu.make_async_copy(r2, idx, lsem)
    tosmem.start()
    tosmem.wait()

    left = lax.broadcasted_iota(jnp.int32, (HALF, 2 * CELLS), 1) < CELLS

    def fill(i, box, at):
        ta, to = moved(i, 1)
        for p in range(PAIRS):
            ia = idx[to, 0, ta * KROWS + 2 * p]
            ib = idx[to, 0, ta * KROWS + 2 * p + 1]
            a = xt[ia]
            b = xt[ib]
            low = jnp.where(left, a, pltpu.roll(b, CELLS, 1))
            high = jnp.where(left, pltpu.roll(a, CELLS, 1), b)
            box[at, p * TF : p * TF + HALF, :] = low.astype(jnp.bfloat16)
            box[at, p * TF + HALF : (p + 1) * TF, :] = high.astype(jnp.bfloat16)
        return ta, to

    fill(0, recv, 0)

    def ship(i, carry):
        ta, to = fill(i, send, i)
        pltpu.make_async_remote_copy(
            send.at[i], recv.at[i], dsend, drecv.at[i // PER],
            device_id=(ta, to), device_id_type=MESH,
        ).start()
        return carry

    for i in range(1, 4):
        ship(i, 0)

    def ship_four(q, carry):
        for i in range(4):
            ship(4 * q + i, 0)
        return carry

    lax.fori_loop(1, OWNERS // 4, ship_four, 0)

    wcopy.wait()
    for p in range(PAIRS):
        def turn_weights(a, carry):
            both = jnp.concatenate([win[2 * p, a], win[2 * p + 1, a]], axis=0).astype(jnp.float32)
            wt[p, pl.ds(a, OWNERS, stride=WPITCH), :] = jnp.transpose(both)
            return carry

        lax.fori_loop(0, CELLS, turn_weights, 0, unroll=8)

    small[1].wait()
    small[2].wait()
    j = lax.broadcasted_iota(jnp.int32, (PAIRS * OWNERS, OWNERS), 0)
    step = (j * 171) >> 9
    pair = j - PAIRS * step
    came = sender_of(step)
    col = lax.broadcasted_iota(jnp.int32, (PAIRS * OWNERS, OWNERS), 1)
    found = jnp.zeros((PAIRS * OWNERS, KROWS), jnp.float32)
    for p in range(PAIRS):
        pick = jnp.where((came == col) & (pair == p), 1.0, 0.0).astype(jnp.bfloat16)
        terms = []
        for par in range(2):
            k = 2 * p + par
            goal = jnp.where(cnt_ref[...] > k, tgt_ref[k] + 1, 0)
            terms += [goal >> 4, goal & 15]
        terms = jnp.concatenate(terms + terms, axis=0).astype(jnp.float32).astype(jnp.bfloat16)
        found += lax.dot_general(
            pick, terms, (((1,), (1,)), ((), ())), preferred_element_type=jnp.float32
        )
    block = lax.broadcasted_iota(jnp.int32, (OWNERS, NBLK), 1).astype(jnp.float32)
    for par in range(2):
        goal = found[:, 2 * par : 2 * par + 1] * 16.0 + found[:, 2 * par + 1 : 2 * par + 2] - 1.0
        for b in range(PAIRS):
            mine = goal[b * OWNERS : (b + 1) * OWNERS]
            ones = jnp.where(block == mine, 1.0, 0.0).astype(jnp.bfloat16)
            for h in range(2):
                if b < PAIRS - 1:
                    at = (2 * h + par) * OWNERS
                    hot[b, at : at + OWNERS, :] = ones
                    continue
                for u in range(2):
                    at = u * 2 * OWNERS + (2 * par + h) * CELLS
                    hot[b, at : at + CELLS, :] = ones[u * CELLS : (u + 1) * CELLS]

    lane = lax.broadcasted_iota(jnp.int32, (CELLS, 2 * CELLS), 1) < CELLS

    def apply(i, carry):
        fa, fo = moved(i, -1)
        s = fa * NOCN + fo
        for p in range(PAIRS):
            w = wt[p, pl.ds(pl.multiple_of(s * WPITCH, 8), CELLS), :]
            w = w.astype(jnp.bfloat16)
            zero = jnp.zeros_like(w)
            square = jnp.concatenate([jnp.where(lane, w, zero), jnp.where(lane, zero, w)], axis=0)
            prod = jnp.dot(recv[i, p * TF : (p + 1) * TF, :], square, preferred_element_type=jnp.float32)
            part[pl.ds(PAIRS * i + p, TF, stride=PAIRS * OWNERS), :] = prod
        return carry

    def turn_parts(b, tf):
        rows = part[pl.ds(tf * PAIRS * OWNERS + b * OWNERS, OWNERS), :]
        rows = jnp.transpose(rows)
        high = rows.astype(jnp.bfloat16)
        low = (rows - high.astype(jnp.float32)).astype(jnp.bfloat16)
        at = pl.ds(tf * CELLS, CELLS)
        for h, term in enumerate((high, low)):
            lhs[at, 2 * h * OWNERS : (2 * h + 1) * OWNERS] = term[:CELLS]
            lhs[at, (2 * h + 1) * OWNERS : (2 * h + 2) * OWNERS] = term[CELLS:]

    def turn_half(u, tf):
        first = (PAIRS - 1) * OWNERS + u * CELLS
        rows = part[pl.ds(tf * PAIRS * OWNERS + first, CELLS), :]
        high = rows.astype(jnp.bfloat16).astype(jnp.float32)
        both = jnp.transpose(jnp.concatenate([high, rows - high], axis=0)).astype(jnp.bfloat16)
        at = pl.ds(tf * CELLS, CELLS)
        lhs[at, :OWNERS] = both[:CELLS]
        lhs[at, OWNERS : 2 * OWNERS] = both[CELLS:]

    def place(n):
        for t in range(TF):
            if n < PAIRS - 1:
                turn_parts(n, t)
            else:
                turn_half(n - PAIRS + 1, t)
        if n < PAIRS - 1:
            more = jnp.dot(lhs[...], hot[n], preferred_element_type=jnp.float32)
        else:
            at = (n - PAIRS + 1) * 2 * OWNERS
            more = jnp.dot(
                lhs[:, : 2 * OWNERS], hot[PAIRS - 1, at : at + 2 * OWNERS, :],
                preferred_element_type=jnp.float32,
            )
        acc[...] = more if n == 0 else acc[...] + more

    ready = [(b + 1) * OWNERS for b in range(PAIRS - 1)]
    ready += [PAIRS * OWNERS - CELLS, PAIRS * OWNERS]
    for g in range(GROUPS):
        n = PER - 1 if g == 0 else PER
        pltpu.make_async_remote_copy(
            send.at[pl.ds(0, n)], recv.at[pl.ds(0, n)], dsend, drecv.at[g],
            device_id=(atm, ocn), device_id_type=MESH,
        ).wait_recv()
        lax.fori_loop(g * PER, (g + 1) * PER, apply, 0, unroll=8)
        for n, bound in enumerate(ready):
            if g * PER * PAIRS < bound <= (g + 1) * PER * PAIRS:
                place(n)

    pltpu.make_async_remote_copy(
        send.at[pl.ds(1, OWNERS - 1)], recv.at[pl.ds(1, OWNERS - 1)], dsend, drecv.at[0],
        device_id=(atm, ocn), device_id_type=MESH,
    ).wait_send()


def exchange(fields, req, mats, targets, counts):
    far = pl.BlockSpec(memory_space=pltpu.HBM)
    return pl.pallas_call(
        exchange_kernel,
        out_shape=pltpu.VMEM((TF * CELLS, NBLK), jnp.float32),
        in_specs=[far] * 5,
        out_specs=pl.BlockSpec(memory_space=pltpu.VMEM),
        scratch_shapes=[
            pltpu.VMEM((CAP, 1, OWNERS), jnp.int32),
            pltpu.VMEM((CAP, 1, OWNERS), jnp.int32),
            pltpu.VMEM((1, OWNERS), jnp.int32),
            pltpu.VMEM((TF, CELLS, NBLK), jnp.bfloat16),
            pltpu.VMEM((CAP, CELLS, CELLS, OWNERS), jnp.bfloat16),
            pltpu.VMEM((NBLK, HALF, 2 * CELLS), jnp.float32),
            pltpu.VMEM((PAIRS, OWNERS * WPITCH, 2 * CELLS), jnp.float32),
            pltpu.VMEM((KROWS, OWNERS), jnp.int32),
            pltpu.VMEM((NATM, KROWS, OWNERS), jnp.int32),
            pltpu.VMEM((OWNERS, OWNERS), jnp.int32),
            pltpu.VMEM((NOCN, 1, OWNERS), jnp.int32),
            pltpu.VMEM((NOCN, 1, OWNERS), jnp.int32),
            pltpu.SMEM((NOCN, 1, OWNERS), jnp.int32),
            pltpu.VMEM((OWNERS, ROWS, 2 * CELLS), jnp.bfloat16),
            pltpu.VMEM((OWNERS, ROWS, 2 * CELLS), jnp.bfloat16),
            pltpu.VMEM((TF * PAIRS * OWNERS, 2 * CELLS), jnp.float32),
            pltpu.VMEM((TF * CELLS, 4 * OWNERS), jnp.bfloat16),
            pltpu.VMEM((PAIRS, 4 * OWNERS, NBLK), jnp.bfloat16),
            pltpu.SemaphoreType.DMA,
            pltpu.SemaphoreType.DMA,
            pltpu.SemaphoreType.DMA,
            pltpu.SemaphoreType.DMA((3,)),
            pltpu.SemaphoreType.DMA,
            pltpu.SemaphoreType.DMA,
            pltpu.SemaphoreType.DMA,
            pltpu.SemaphoreType.DMA,
            pltpu.SemaphoreType.DMA,
            pltpu.SemaphoreType.DMA((GROUPS,)),
        ],
        compiler_params=pltpu.CompilerParams(
            collective_id=0, has_side_effects=True, vmem_limit_bytes=56 << 20
        ),
        name="exchange",
    )(fields, req, mats, targets, counts)


def on_device(atm_fields, requests, ocean_block, live_counts, weights):
    fields = jnp.transpose(atm_fields, (1, 2, 3, 0)).reshape(TF, CELLS, NBLK)
    req = jnp.transpose(requests, (2, 0, 1))
    targets = jnp.transpose(ocean_block, (2, 0, 1))
    mats = jnp.transpose(weights[0], (1, 2, 3, 0))
    out = exchange(fields, req, mats, targets, live_counts)
    return jnp.transpose(out.reshape(4, 8, CELLS, NBLK), (3, 0, 1, 2))


def solution(mesh):
    in_specs = (
        P(("atm", "ocn"), None, None, None),
        P(("atm", "ocn"), None, None),
        P(("atm", "ocn"), None, None),
        P(("atm", "ocn"), None),
        P(("atm", "ocn"), None, None, None, None),
    )
    out_specs = P(("atm", "ocn"), None, None, None)
    return jax.shard_map(
        on_device, mesh=mesh, in_specs=in_specs, out_specs=out_specs, check_vma=False
    )
```

```python
import jax
import jax.numpy as jnp
from jax import lax
from jax.experimental import pallas as pl
from jax.experimental.pallas import tpu as pltpu
from jax.sharding import PartitionSpec as P

MESH = pl.DeviceIdType.MESH
OWNERS = 128
NATM = 8
NOCN = 16
CAP = 6
KROWS = 8
PAIRS = 3
CELLS = 64
TF = 32
HALF = 16
NBLK = 512
GROUPS = 32
PER = OWNERS // GROUPS
ROWS = PAIRS * TF
WPITCH = CELLS


def shift_of(i):
    j = (i * 91) % OWNERS
    return j // 32, (j // 16) % 2, (j // 4) % 4, j % 4


def moved(i, sign):
    atm = lax.axis_index("atm")
    ocn = lax.axis_index("ocn")
    dy, dc, dx, dz = shift_of(i)
    y = (atm // 2 + 4 + sign * dy) % 4
    c = (atm % 2 + 2 + sign * dc) % 2
    x = (ocn // 4 + 4 + sign * dx) % 4
    z = (ocn % 4 + 4 + sign * dz) % 4
    return y * 2 + c, x * 4 + z


def sender_of(i):
    atm = lax.axis_index("atm")
    ocn = lax.axis_index("ocn")
    j = (i * 91) & (OWNERS - 1)
    y = (atm // 2 - (j >> 5)) & 3
    c = (atm % 2 - (j >> 4)) & 1
    x = (ocn // 4 - (j >> 2)) & 3
    z = (ocn % 4 - j) & 3
    return ((y * 2 + c) * 4 + x) * 4 + z


def exchange_kernel(
    x_hbm, req_hbm, w_hbm, tgt_hbm, cnt_hbm, acc,
    req_ref, tgt_ref, cnt_ref, xin, win, xt, wt, reqm, r1, turned, rows, r2, idx, send, recv, part, lhs, hot,
    xsem, wsem, lsem, isem, s1, v1, s2, v2, dsend, drecv,
):
    atm = lax.axis_index("atm")
    ocn = lax.axis_index("ocn")
    small = [
        pltpu.make_async_copy(a, b, isem.at[n])
        for n, (a, b) in enumerate(((req_hbm, req_ref), (tgt_hbm, tgt_ref), (cnt_hbm, cnt_ref)))
    ]
    for copy in small:
        copy.start()
    xcopy = pltpu.make_async_copy(x_hbm, xin, xsem)
    xcopy.start()
    wcopy = pltpu.make_async_copy(w_hbm, win, wsem)
    wcopy.start()

    barrier = pltpu.get_barrier_semaphore()

    for i in range(1, NATM):
        pl.semaphore_signal(barrier, inc=1, device_id=((atm + i) % NATM, ocn), device_id_type=MESH)
    for i in range(1, NOCN):
        pl.semaphore_signal(barrier, inc=1, device_id=(atm, (ocn + i) % NOCN), device_id_type=MESH)
    small[0].wait()
    for k in range(CAP):
        reqm[k : k + 1, :] = req_ref[k] & (NBLK - 1)
    reqm[CAP:, :] = jnp.zeros((KROWS - CAP, OWNERS), jnp.int32)

    pl.semaphore_wait(barrier, NATM + NOCN - 2)

    for i in range(1, NATM):
        pltpu.make_async_remote_copy(
            reqm, r1.at[atm], s1, v1, device_id=((atm + i) % NATM, ocn), device_id_type=MESH
        ).start()
    r1[atm] = reqm[...]

    xcopy.wait()
    xflat = xt.reshape(NBLK * HALF, 2 * CELLS)

    def turn_fields(tp, carry):
        both = jnp.concatenate([xin[tp], xin[tp + HALF]], axis=0).astype(jnp.float32)
        for b in range(0, NBLK, 128):
            xflat[pl.ds(b * HALF + tp, 128, stride=HALF), :] = jnp.transpose(both[:, b : b + 128])
        return carry

    lax.fori_loop(0, HALF // 2, turn_fields, 0)

    hop1 = pltpu.make_async_remote_copy(
        r1.at[pl.ds(0, NATM - 1)], r1.at[pl.ds(0, NATM - 1)], s1, v1,
        device_id=(atm, ocn), device_id_type=MESH,
    )
    hop1.wait_recv()
    half = r1[...].reshape(NATM * KROWS, OWNERS)
    turned[...] = jnp.transpose(jnp.concatenate([half, half], axis=0))
    mine = turned[pl.ds(pl.multiple_of(atm * NOCN, NOCN), NOCN), :]
    for o in range(NOCN):
        rows[o] = mine[o : o + 1, :]

    for i in range(1, NOCN):
        to = (ocn + i) % NOCN
        pltpu.make_async_remote_copy(
            rows.at[to], r2.at[ocn], s2, v2, device_id=(atm, to), device_id_type=MESH
        ).start()
    r2[ocn] = rows[ocn]

    lax.fori_loop(HALF // 2, HALF, turn_fields, 0)

    hop1.wait_send()
    hop2 = pltpu.make_async_remote_copy(
        r2.at[pl.ds(0, NOCN - 1)], r2.at[pl.ds(0, NOCN - 1)], s2, v2,
        device_id=(atm, ocn), device_id_type=MESH,
    )
    hop2.wait_recv()
    hop2.wait_send()
    tosmem = pltpu.make_async_copy(r2, idx, lsem)
    tosmem.start()
    tosmem.wait()

    left = lax.broadcasted_iota(jnp.int32, (HALF, 2 * CELLS), 1) < CELLS

    def fill(i, box, at):
        ta, to = moved(i, 1)
        for p in range(PAIRS):
            ia = idx[to, 0, ta * KROWS + 2 * p]
            ib = idx[to, 0, ta * KROWS + 2 * p + 1]
            a = xt[ia]
            b = xt[ib]
            low = jnp.where(left, a, pltpu.roll(b, CELLS, 1))
            high = jnp.where(left, pltpu.roll(a, CELLS, 1), b)
            box[at, p * TF : p * TF + HALF, :] = low.astype(jnp.bfloat16)
            box[at, p * TF + HALF : (p + 1) * TF, :] = high.astype(jnp.bfloat16)
        return ta, to

    fill(0, recv, 0)

    def ship(i, carry):
        ta, to = fill(i, send, i)
        pltpu.make_async_remote_copy(
            send.at[i], recv.at[i], dsend, drecv.at[i // PER],
            device_id=(ta, to), device_id_type=MESH,
        ).start()
        return carry

    for i in range(1, 4):
        ship(i, 0)

    def ship_four(q, carry):
        for i in range(4):
            ship(4 * q + i, 0)
        return carry

    lax.fori_loop(1, OWNERS // 4, ship_four, 0)

    wcopy.wait()
    for p in range(PAIRS):
        def turn_weights(a, carry):
            both = jnp.concatenate([win[2 * p, a], win[2 * p + 1, a]], axis=0).astype(jnp.float32)
            wt[p, pl.ds(a, OWNERS, stride=WPITCH), :] = jnp.transpose(both)
            return carry

        lax.fori_loop(0, CELLS, turn_weights, 0, unroll=8)

    small[1].wait()
    small[2].wait()
    j = lax.broadcasted_iota(jnp.int32, (PAIRS * OWNERS, OWNERS), 0)
    step = (j * 171) >> 9
    pair = j - PAIRS * step
    came = sender_of(step)
    col = lax.broadcasted_iota(jnp.int32, (PAIRS * OWNERS, OWNERS), 1)
    found = jnp.zeros((PAIRS * OWNERS, KROWS), jnp.float32)
    for p in range(PAIRS):
        pick = jnp.where((came == col) & (pair == p), 1.0, 0.0).astype(jnp.bfloat16)
        terms = []
        for par in range(2):
            k = 2 * p + par
            goal = jnp.where(cnt_ref[...] > k, tgt_ref[k] + 1, 0)
            terms += [goal >> 4, goal & 15]
        terms = jnp.concatenate(terms + terms, axis=0).astype(jnp.float32).astype(jnp.bfloat16)
        found += lax.dot_general(
            pick, terms, (((1,), (1,)), ((), ())), preferred_element_type=jnp.float32
        )
    block = lax.broadcasted_iota(jnp.int32, (OWNERS, NBLK), 1).astype(jnp.float32)
    for par in range(2):
        goal = found[:, 2 * par : 2 * par + 1] * 16.0 + found[:, 2 * par + 1 : 2 * par + 2] - 1.0
        for b in range(PAIRS):
            mine = goal[b * OWNERS : (b + 1) * OWNERS]
            ones = jnp.where(block == mine, 1.0, 0.0).astype(jnp.bfloat16)
            for h in range(2):
                if b < PAIRS - 1:
                    at = (2 * h + par) * OWNERS
                    hot[b, at : at + OWNERS, :] = ones
                    continue
                for u in range(2):
                    at = u * 2 * OWNERS + (2 * par + h) * CELLS
                    hot[b, at : at + CELLS, :] = ones[u * CELLS : (u + 1) * CELLS]

    lane = lax.broadcasted_iota(jnp.int32, (CELLS, 2 * CELLS), 1) < CELLS

    def apply(i, carry):
        fa, fo = moved(i, -1)
        s = fa * NOCN + fo
        for p in range(PAIRS):
            w = wt[p, pl.ds(pl.multiple_of(s * WPITCH, 8), CELLS), :]
            w = w.astype(jnp.bfloat16)
            zero = jnp.zeros_like(w)
            square = jnp.concatenate([jnp.where(lane, w, zero), jnp.where(lane, zero, w)], axis=0)
            prod = jnp.dot(recv[i, p * TF : (p + 1) * TF, :], square, preferred_element_type=jnp.float32)
            part[pl.ds(PAIRS * i + p, TF, stride=PAIRS * OWNERS), :] = prod
        return carry

    def turn_parts(b, tf):
        rows = part[pl.ds(tf * PAIRS * OWNERS + b * OWNERS, OWNERS), :]
        rows = jnp.transpose(rows)
        high = rows.astype(jnp.bfloat16)
        low = (rows - high.astype(jnp.float32)).astype(jnp.bfloat16)
        at = pl.ds(tf * CELLS, CELLS)
        for h, term in enumerate((high, low)):
            lhs[at, 2 * h * OWNERS : (2 * h + 1) * OWNERS] = term[:CELLS]
            lhs[at, (2 * h + 1) * OWNERS : (2 * h + 2) * OWNERS] = term[CELLS:]

    def turn_half(u, tf):
        first = (PAIRS - 1) * OWNERS + u * CELLS
        rows = part[pl.ds(tf * PAIRS * OWNERS + first, CELLS), :]
        high = rows.astype(jnp.bfloat16).astype(jnp.float32)
        both = jnp.transpose(jnp.concatenate([high, rows - high], axis=0)).astype(jnp.bfloat16)
        at = pl.ds(tf * CELLS, CELLS)
        lhs[at, :OWNERS] = both[:CELLS]
        lhs[at, OWNERS : 2 * OWNERS] = both[CELLS:]

    def place(n):
        for t in range(TF):
            if n < PAIRS - 1:
                turn_parts(n, t)
            else:
                turn_half(n - PAIRS + 1, t)
        if n < PAIRS - 1:
            more = jnp.dot(lhs[...], hot[n], preferred_element_type=jnp.float32)
        else:
            at = (n - PAIRS + 1) * 2 * OWNERS
            more = jnp.dot(
                lhs[:, : 2 * OWNERS], hot[PAIRS - 1, at : at + 2 * OWNERS, :],
                preferred_element_type=jnp.float32,
            )
        acc[...] = more if n == 0 else acc[...] + more

    ready = [(b + 1) * OWNERS for b in range(PAIRS - 1)]
    ready += [PAIRS * OWNERS - CELLS, PAIRS * OWNERS]
    for g in range(GROUPS):
        n = PER - 1 if g == 0 else PER
        pltpu.make_async_remote_copy(
            send.at[pl.ds(0, n)], recv.at[pl.ds(0, n)], dsend, drecv.at[g],
            device_id=(atm, ocn), device_id_type=MESH,
        ).wait_recv()
        lax.fori_loop(g * PER, (g + 1) * PER, apply, 0, unroll=4)
        for n, bound in enumerate(ready):
            if g * PER * PAIRS < bound <= (g + 1) * PER * PAIRS:
                place(n)

    pltpu.make_async_remote_copy(
        send.at[pl.ds(1, OWNERS - 1)], recv.at[pl.ds(1, OWNERS - 1)], dsend, drecv.at[0],
        device_id=(atm, ocn), device_id_type=MESH,
    ).wait_send()


def exchange(fields, req, mats, targets, counts):
    far = pl.BlockSpec(memory_space=pltpu.HBM)
    return pl.pallas_call(
        exchange_kernel,
        out_shape=pltpu.VMEM((TF * CELLS, NBLK), jnp.float32),
        in_specs=[far] * 5,
        out_specs=pl.BlockSpec(memory_space=pltpu.VMEM),
        scratch_shapes=[
            pltpu.VMEM((CAP, 1, OWNERS), jnp.int32),
            pltpu.VMEM((CAP, 1, OWNERS), jnp.int32),
            pltpu.VMEM((1, OWNERS), jnp.int32),
            pltpu.VMEM((TF, CELLS, NBLK), jnp.bfloat16),
            pltpu.VMEM((CAP, CELLS, CELLS, OWNERS), jnp.bfloat16),
            pltpu.VMEM((NBLK, HALF, 2 * CELLS), jnp.float32),
            pltpu.VMEM((PAIRS, OWNERS * WPITCH, 2 * CELLS), jnp.float32),
            pltpu.VMEM((KROWS, OWNERS), jnp.int32),
            pltpu.VMEM((NATM, KROWS, OWNERS), jnp.int32),
            pltpu.VMEM((OWNERS, OWNERS), jnp.int32),
            pltpu.VMEM((NOCN, 1, OWNERS), jnp.int32),
            pltpu.VMEM((NOCN, 1, OWNERS), jnp.int32),
            pltpu.SMEM((NOCN, 1, OWNERS), jnp.int32),
            pltpu.VMEM((OWNERS, ROWS, 2 * CELLS), jnp.bfloat16),
            pltpu.VMEM((OWNERS, ROWS, 2 * CELLS), jnp.bfloat16),
            pltpu.VMEM((TF * PAIRS * OWNERS, 2 * CELLS), jnp.float32),
            pltpu.VMEM((TF * CELLS, 4 * OWNERS), jnp.bfloat16),
            pltpu.VMEM((PAIRS, 4 * OWNERS, NBLK), jnp.bfloat16),
            pltpu.SemaphoreType.DMA,
            pltpu.SemaphoreType.DMA,
            pltpu.SemaphoreType.DMA,
            pltpu.SemaphoreType.DMA((3,)),
            pltpu.SemaphoreType.DMA,
            pltpu.SemaphoreType.DMA,
            pltpu.SemaphoreType.DMA,
            pltpu.SemaphoreType.DMA,
            pltpu.SemaphoreType.DMA,
            pltpu.SemaphoreType.DMA((GROUPS,)),
        ],
        compiler_params=pltpu.CompilerParams(
            collective_id=0, has_side_effects=True, vmem_limit_bytes=56 << 20
        ),
        name="exchange",
    )(fields, req, mats, targets, counts)


def on_device(atm_fields, requests, ocean_block, live_counts, weights):
    fields = jnp.transpose(atm_fields, (1, 2, 3, 0)).reshape(TF, CELLS, NBLK)
    req = jnp.transpose(requests, (2, 0, 1))
    targets = jnp.transpose(ocean_block, (2, 0, 1))
    mats = jnp.transpose(weights[0], (1, 2, 3, 0))
    out = exchange(fields, req, mats, targets, live_counts)
    return jnp.transpose(out.reshape(4, 8, CELLS, NBLK), (3, 0, 1, 2))


def solution(mesh):
    in_specs = (
        P(("atm", "ocn"), None, None, None),
        P(("atm", "ocn"), None, None),
        P(("atm", "ocn"), None, None),
        P(("atm", "ocn"), None),
        P(("atm", "ocn"), None, None, None, None),
    )
    out_specs = P(("atm", "ocn"), None, None, None)
    return jax.shard_map(
        on_device, mesh=mesh, in_specs=in_specs, out_specs=out_specs, check_vma=False
    )
```
